32 devices in a mesh: grp: 2 (over core), seq: 4 (over z), mdl: 4 (over y, x).
Axes of the slice: x: 2, y: 2, z: 4, core: 2. Of those that a mesh axis runs over, the one named last changes fastest.
Arguments:
- queries: bfloat16 [512, 8, 2048], P(('grp', 'seq'), None, 'mdl'), may hold values from -7 to 7
- out_grads: bfloat16 [512, 8, 2048], P(('grp', 'seq'), None, 'mdl'), may hold values from -12 to 12
- owners: int32 [512], P(('grp', 'seq')), may hold values from 0 to 7, as said below
- src_keys: bfloat16 [8, 512, 2048], P(('grp', 'seq'), None, 'mdl'), may hold values from -7 to 7
- src_values: bfloat16 [8, 512, 2048], P(('grp', 'seq'), None, 'mdl'), may hold values from -6 to 6
- states: bfloat16 [8, 512, 2048], P(('grp', 'seq'), None, 'mdl'), may hold values from -0.59765625 to 0.59765625
- kv_weight: bfloat16 [2048, 2, 2048], P(('grp', 'seq'), None, 'mdl'), may hold values from -0.125 to 0.125
- src_lengths: int32 [8], P(('grp', 'seq')), may hold values from 128 to 512, as said below
Outputs:
- query_grads: bfloat16 [512, 8, 2048], P(('grp', 'seq'), None, 'mdl')
- state_grads: bfloat16 [8, 512, 2048], P(('grp', 'seq'), None, 'mdl')
- weight_grads: float32 [2048, 2, 2048], P(('grp', 'seq'), None, 'mdl')
The draws below stay inside these ranges and needn't reach their ends.
Inputs may be any that keep to these rules, and one draw needn't show every extreme that they name: `owners`: the 64 targets of each index of grp and seq (an aligned block) name any one source at most 16 times; one source, the same for every block, is named exactly 16 times by every block. `src_lengths`: each length is a multiple of 128; the largest is 512.
All inputs are finite; a program needn't handle non-finite values.
Results may differ from the reference program's by a relative error of at most 0.012.
Values may be sent and summed in bfloat16 or wider, within the bound.
No kernel may reach another device: no remote copies, remote signals or barrier semaphores. Data moves between devices by JAX's collectives and lax.ppermute only.
A program may use at most 64 MiB of HBM per device.

```python
import jax
import jax.numpy as jnp
from jax import lax

D = 2048
HEADS = 32
HEAD_DIM = 64
INNER = 2048
SRC = 512
TGT = 8
TGT_DEV = 64
SOURCES = 8
TARGETS = 512
MOST = 16


def draw_queries(key, part):
    inner_key = jax.random.fold_in(key, 11)
    shape = (TARGETS, TGT, HEADS, HEAD_DIM)
    values = jnp.clip(jax.random.normal(inner_key, shape, jnp.float32), -4.0, 4.0)
    return values.reshape(TARGETS, TGT, INNER).astype(jnp.bfloat16)


def draw_src_keys(key, part):
    inner_key = jax.random.fold_in(key, 23)
    shape = (SOURCES, SRC, HEADS, HEAD_DIM)
    values = jnp.clip(jax.random.normal(inner_key, shape, jnp.float32), -4.0, 4.0)
    return values.reshape(SOURCES, SRC, INNER).astype(jnp.bfloat16)


def draw_owners(key, part):
    busiest = jax.random.randint(jax.random.fold_in(key, 5), (), 0, SOURCES)

    def one_block(block_id):
        block_key = jax.random.fold_in(key, 100 + block_id)
        pool = jnp.arange((SOURCES - 1) * MOST, dtype=jnp.int32) // MOST
        pool = jax.random.permutation(jax.random.fold_in(block_key, 1), pool)
        others = pool[:TGT_DEV - MOST]
        others = others + (others >= busiest).astype(jnp.int32)
        names = jnp.concatenate([jnp.full((MOST,), busiest, jnp.int32), others.astype(jnp.int32)])
        order = jax.random.permutation(jax.random.fold_in(block_key, 2), TGT_DEV)
        return names[order]
    return jax.vmap(one_block)(jnp.arange(SOURCES, dtype=jnp.int32)).reshape(TARGETS).astype(jnp.int32)


def draw_src_lengths(key, part):
    blocks = jax.random.randint(jax.random.fold_in(key, 7), (SOURCES,), 1, SRC // 128 + 1)
    longest = jax.random.randint(jax.random.fold_in(key, 8), (), 0, SOURCES)
    blocks = jnp.where(jnp.arange(SOURCES, dtype=jnp.int32) == longest, SRC // 128, blocks)
    return (blocks * 128).astype(jnp.int32)


def block_scale(key, dims, pieces, least, top_value):
    factor_of, own = 1.0, jax.random.fold_in(key, 6)
    for dim, parts in pieces:
        draws = jnp.exp(jax.random.uniform(jax.random.fold_in(own, dim), (parts,), jnp.float32, least / len(pieces), top_value / len(pieces)))
        factor_of = factor_of * jnp.repeat(draws, dims[dim] // parts).reshape([-1 if axis == dim else 1 for axis in range(len(dims))])
    return factor_of


def noise(key, extent, deviation, limit, split=(), kind=jnp.bfloat16):
    values = deviation * jax.random.normal(key, extent, jnp.float32)
    if split:
        values = values * block_scale(key, extent, split, -0.22, 0.18)
    return jnp.clip(values, -limit, limit).astype(kind)


def setup_inputs(seed: int = 0) -> dict:
    arg_keys = jax.random.split(jax.random.key(seed), 9)
    return {
        "queries": draw_queries(jax.random.fold_in(arg_keys[8], 71), 0),
        "out_grads": noise(arg_keys[1], (TARGETS, TGT, INNER), 2.0, 12.0, ((0, 8), (2, 4))),
        "owners": draw_owners(jax.random.fold_in(arg_keys[8], 71), 0),
        "src_keys": draw_src_keys(jax.random.fold_in(arg_keys[8], 71), 0),
        "src_values": noise(arg_keys[4], (SOURCES, SRC, INNER), 1.0, 6.0, ((0, 8), (2, 4))),
        "states": noise(arg_keys[5], (SOURCES, SRC, D), 0.1, 0.59765625, ((0, 8), (2, 4))),
        "kv_weight": noise(arg_keys[6], (INNER, 2, D), INNER ** -0.5, 0.125, ((0, 8), (2, 4))),
        "src_lengths": draw_src_lengths(jax.random.fold_in(arg_keys[8], 71), 0),
    }


def block_grads(query_block, grad_block, key_block, value_block, key_valid):
    score_scale = HEAD_DIM ** -0.5
    query_f = query_block.astype(jnp.float32)
    grad_f = grad_block.astype(jnp.float32)
    key_f = key_block.astype(jnp.float32)
    value_f = value_block.astype(jnp.float32)
    scores = jnp.einsum('bqhe,bkhe->bhqk', query_f, key_f) * score_scale
    scores = jnp.where(key_valid[:, None, None, :], scores, -1e30)
    row_peak = jnp.max(scores, axis=-1, keepdims=True)
    exp_terms = jnp.exp(scores - row_peak)
    attn_probs = exp_terms / jnp.sum(exp_terms, axis=-1, keepdims=True)
    probs_b = lax.optimization_barrier(attn_probs.astype(jnp.bfloat16))
    probs_back = probs_b.astype(jnp.float32)
    context = jnp.einsum('bhqk,bkhe->bqhe', probs_back, value_f)
    row_delta = jnp.sum(grad_f * context, axis=-1)
    prob_grad = jnp.einsum('bqhe,bkhe->bhqk', grad_f, value_f)
    centred = prob_grad - jnp.transpose(row_delta, (0, 2, 1))[..., None]
    score_grad = lax.optimization_barrier((attn_probs * centred * score_scale).astype(jnp.bfloat16))
    score_back = score_grad.astype(jnp.float32)
    query_grad = jnp.einsum('bhqk,bkhe->bqhe', score_back, key_f).astype(jnp.bfloat16)
    key_grad = jnp.einsum('bhqk,bqhe->bkhe', score_back, query_f)
    value_grad = jnp.einsum('bhqk,bqhe->bkhe', probs_back, grad_f)
    return query_grad, key_grad, value_grad


def reference(queries, out_grads, owners, src_keys, src_values, states, kv_weight, src_lengths):
    query_all = queries.reshape(SOURCES, TGT_DEV, TGT, HEADS, HEAD_DIM)
    grad_all = out_grads.reshape(SOURCES, TGT_DEV, TGT, HEADS, HEAD_DIM)
    owner_all = owners.reshape(SOURCES, TGT_DEV).astype(jnp.int32)
    key_all = src_keys.reshape(SOURCES, SRC, HEADS, HEAD_DIM)
    value_all = src_values.reshape(SOURCES, SRC, HEADS, HEAD_DIM)
    positions = jnp.arange(SRC, dtype=jnp.int32)

    def attend_step(totals, block_pair):
        query_block, grad_block, owner_block = block_pair
        key_block = key_all[owner_block]
        value_block = value_all[owner_block]
        key_valid = positions[None, :] < src_lengths[owner_block][:, None]
        query_grad, key_grad, value_grad = block_grads(query_block, grad_block, key_block, value_block, key_valid)
        key_total = totals[0].at[owner_block].add(key_grad)
        value_total = totals[1].at[owner_block].add(value_grad)
        return (key_total, value_total), query_grad

    zero_grads = jnp.zeros((SOURCES, SRC, HEADS, HEAD_DIM), jnp.float32)
    (key_total, value_total), query_out = lax.scan(attend_step, (zero_grads, zero_grads), (query_all, grad_all, owner_all))
    query_grads = query_out.reshape(TARGETS, TGT, INNER)
    key_flat = key_total.astype(jnp.bfloat16).reshape(SOURCES * SRC, INNER)
    value_flat = value_total.astype(jnp.bfloat16).reshape(SOURCES * SRC, INNER)
    state_sum = jnp.dot(key_flat, kv_weight[:, 0, :], preferred_element_type=jnp.float32)
    state_sum = state_sum + jnp.dot(value_flat, kv_weight[:, 1, :], preferred_element_type=jnp.float32)
    state_grads = state_sum.astype(jnp.bfloat16).reshape(SOURCES, SRC, D)
    flat_states = states.reshape(SOURCES * SRC, D)
    grad_key = lax.dot_general(key_flat, flat_states, (((0,), (0,)), ((), ())), preferred_element_type=jnp.float32)
    grad_value = lax.dot_general(value_flat, flat_states, (((0,), (0,)), ((), ())), preferred_element_type=jnp.float32)
    weight_grads = jnp.stack([grad_key, grad_value], axis=1)
    return (query_grads, state_grads, weight_grads)
```

```python
import functools

import jax
import jax.numpy as jnp
from jax import lax
from jax.experimental import pallas as pl
from jax.experimental.pallas import tpu as pltpu
from jax.sharding import PartitionSpec as P

HEAD_DIM = 64
LANES = 128
PEERS = ("grp", "seq")
BF16 = jnp.bfloat16
F32 = jnp.float32
VMEM_BYTES = 40 * 1024 * 1024

VMEM_SPEC = pl.BlockSpec(memory_space=pltpu.VMEM)
SMEM_SPEC = pl.BlockSpec(memory_space=pltpu.SMEM)
NT = (((1,), (1,)), ((), ()))
TN = (((0,), (0,)), ((), ()))


def cost(flops, bytes_accessed, transcendentals=0):
    return pl.CostEstimate(
        flops=flops, bytes_accessed=bytes_accessed, transcendentals=transcendentals
    )


def pack_kernel(peers, per_peer, chunks, me_ref, owners_ref, q_ref, g_ref, *refs):
    table_ref, out_refs = refs[0], refs[1 : 1 + chunks * peers]
    both_ref, count_ref = refs[-2:]
    targets, rows, width = q_ref.shape
    both = jnp.concatenate([q_ref[...].astype(F32), g_ref[...].astype(F32)], axis=1)
    both_ref[:targets] = both.astype(BF16)
    both_ref[targets] = jnp.zeros((2 * rows, width), BF16)
    me = me_ref[0]

    def clear_count(i, _):
        count_ref[i] = 0
        return 0

    def clear_slot(i, _):
        table_ref[i] = targets
        return 0

    def place(t, _):
        distance = owners_ref[t] ^ me
        rank = count_ref[distance]
        table_ref[distance * per_peer + rank] = t
        count_ref[distance] = rank + 1
        return 0

    lax.fori_loop(0, peers, clear_count, 0)
    lax.fori_loop(0, peers * per_peer, clear_slot, 0)
    lax.fori_loop(0, targets, place, 0)
    groups = width // (chunks * LANES)
    for d in range(peers):

        def move(slot, _, d=d):
            t = table_ref[d * per_peer + slot]
            for c in range(chunks):
                for a in range(groups):
                    lane = (a * chunks + c) * LANES
                    out_refs[c * peers + d][slot, :, a * LANES : (a + 1) * LANES] = both_ref[
                        t, :, lane : lane + LANES
                    ]
            return 0

        lax.fori_loop(0, per_peer, move, 0, unroll=4)


def pack(me, owners, queries, out_grads, peers, per_peer, chunks):
    targets, rows, width = queries.shape
    block = jax.ShapeDtypeStruct((per_peer, 2 * rows, width // chunks), BF16)
    outs = pl.pallas_call(
        functools.partial(pack_kernel, peers, per_peer, chunks),
        out_shape=[jax.ShapeDtypeStruct((peers * per_peer,), jnp.int32)]
        + [block] * (chunks * peers),
        in_specs=[SMEM_SPEC, SMEM_SPEC, VMEM_SPEC, VMEM_SPEC],
        out_specs=[SMEM_SPEC] + [VMEM_SPEC] * (chunks * peers),
        scratch_shapes=[
            pltpu.VMEM((targets + 1, 2 * rows, width), BF16),
            pltpu.SMEM((peers,), jnp.int32),
        ],
        compiler_params=pltpu.CompilerParams(vmem_limit_bytes=VMEM_BYTES),
        cost_estimate=cost(0, 3 << 20),
        name="pack_targets",
    )(me, owners, queries, out_grads)
    return outs[0], [outs[1 + c * peers : 1 + (c + 1) * peers] for c in range(chunks)]


def unpack_kernel(peers, per_peer, chunks, table_ref, *refs):
    in_refs, out_ref, rows_ref = refs[: chunks * peers], refs[-2], refs[-1]
    targets, rows, width = out_ref.shape
    groups = width // (chunks * LANES)
    for c in range(chunks):
        for d in range(peers):
            block = in_refs[c * peers + d][...].astype(F32)
            block = block.reshape(per_peer, rows, width // chunks)
            for a in range(groups):
                lane = (a * chunks + c) * LANES
                rows_ref[d * per_peer : (d + 1) * per_peer, :, lane : lane + LANES] = block[
                    :, :, a * LANES : (a + 1) * LANES
                ]

    def move(slot, _):
        t = table_ref[slot]

        @pl.when(t < targets)
        def _():
            out_ref[t] = rows_ref[slot].astype(BF16)

        return 0

    lax.fori_loop(0, peers * per_peer, move, 0)


def unpack(table, blocks, targets, rows, width, peers, per_peer):
    chunks = len(blocks)
    return pl.pallas_call(
        functools.partial(unpack_kernel, peers, per_peer, chunks),
        out_shape=jax.ShapeDtypeStruct((targets, rows, width), BF16),
        in_specs=[SMEM_SPEC] + [VMEM_SPEC] * (chunks * peers),
        out_specs=VMEM_SPEC,
        scratch_shapes=[pltpu.VMEM((peers * per_peer, rows, width), F32)],
        compiler_params=pltpu.CompilerParams(vmem_limit_bytes=VMEM_BYTES),
        cost_estimate=cost(0, 3 << 20),
        name="unpack_query_grads",
    )(table, *[b for part in blocks for b in part])


def attend_kernel(peers, chunk, chunks, len_ref, k_ref, v_ref, *refs):
    in_refs = refs[:peers]
    groups = k_ref.shape[1] // (chunks * LANES)
    kv_refs = refs[peers : peers + groups]
    out_refs = refs[peers + groups : 2 * peers + groups]
    q_s, g_s, o_s, kt_s, kg_s, vg_s = refs[2 * peers + groups :]
    src_len = k_ref.shape[0]
    per_peer, double, width = in_refs[0].shape
    rows = double // 2
    block_rows = per_peer * rows
    total_rows = peers * block_rows
    tile = min(256, total_rows)
    scale = HEAD_DIM**-0.5
    for d in range(peers):
        both = in_refs[d][...].astype(F32)
        at = slice(d * block_rows, (d + 1) * block_rows)
        q_s[at] = (both[:, :rows] * scale).reshape(block_rows, width).astype(BF16)
        g_s[at] = both[:, rows:].reshape(block_rows, width).astype(BF16)
    valid = lax.broadcasted_iota(jnp.int32, (src_len, 1), 0) < len_ref[0]
    lane_head = lax.broadcasted_iota(jnp.int32, (1, LANES), 1) // HEAD_DIM
    for a in range(groups):
        lane = (a * chunks + chunk) * LANES
        mine = slice(a * LANES, (a + 1) * LANES)
        kt_s[...] = (k_ref[:, lane : lane + LANES].astype(F32) * scale).T.astype(BF16)
        kg_s[...] = jnp.zeros_like(kg_s)
        vg_s[...] = jnp.zeros_like(vg_s)

        def step(i, _, lane=lane, mine=mine):
            at = pl.ds(pl.multiple_of(i * tile, tile), tile)
            q_pair, g_pair = q_s[at, mine], g_s[at, mine]
            k_pair, v_pair = k_ref[:, lane : lane + LANES], v_ref[:, lane : lane + LANES]
            parts = []
            for h in range(LANES // HEAD_DIM):
                q_h = jnp.where(lane_head == h, q_pair, jnp.zeros_like(q_pair))
                g_h = jnp.where(lane_head == h, g_pair, jnp.zeros_like(g_pair))
                scores = lax.dot_general(k_pair, q_h, NT, preferred_element_type=F32)
                scores = jnp.where(valid, scores, -1e30)
                prob_grad = lax.dot_general(v_pair, g_h, NT, preferred_element_type=F32)
                peak = jnp.max(scores, axis=0, keepdims=True)
                terms = jnp.exp(scores - peak)
                probs = terms * (1.0 / jnp.sum(terms, axis=0, keepdims=True))
                row_delta = jnp.sum(probs * prob_grad, axis=0, keepdims=True)
                score_grad = (probs * (prob_grad - row_delta)).astype(BF16)
                vg_s[...] += jnp.dot(probs.astype(BF16), g_h, preferred_element_type=F32)
                kg_s[...] += jnp.dot(score_grad, q_h, preferred_element_type=F32)
                parts.append(
                    jnp.dot(
                        kt_s[h * HEAD_DIM : (h + 1) * HEAD_DIM],
                        score_grad,
                        preferred_element_type=F32,
                    )
                )
            o_s[at, mine] = jnp.concatenate(parts, axis=0).T.astype(BF16)
            return 0

        lax.fori_loop(0, total_rows // tile, step, 0)
        kv_refs[a][:, :LANES] = kg_s[...].astype(BF16)
        kv_refs[a][:, LANES:] = vg_s[...].astype(BF16)
    for d in range(peers):
        out_refs[d][...] = o_s[d * block_rows : (d + 1) * block_rows]


def attend(length, keys, values, blocks, chunk, chunks):
    peers = len(blocks)
    src_len, width = keys.shape
    per_peer, double, part = blocks[0].shape
    block_rows = per_peer * double // 2
    total_rows = peers * block_rows
    groups = part // LANES
    heads = part // HEAD_DIM
    outs = pl.pallas_call(
        functools.partial(attend_kernel, peers, chunk, chunks),
        out_shape=[jax.ShapeDtypeStruct((src_len, 2 * LANES), BF16)] * groups
        + [jax.ShapeDtypeStruct((block_rows, part), BF16)] * peers,
        in_specs=[SMEM_SPEC] + [VMEM_SPEC] * (2 + peers),
        out_specs=[VMEM_SPEC] * (groups + peers),
        scratch_shapes=[
            pltpu.VMEM((total_rows, part), BF16),
            pltpu.VMEM((total_rows, part), BF16),
            pltpu.VMEM((total_rows, part), BF16),
            pltpu.VMEM((LANES, src_len), BF16),
            pltpu.VMEM((src_len, LANES), F32),
            pltpu.VMEM((src_len, LANES), F32),
        ],
        compiler_params=pltpu.CompilerParams(vmem_limit_bytes=VMEM_BYTES),
        cost_estimate=cost(
            40 * total_rows * src_len * HEAD_DIM * heads, 4 << 20, total_rows * src_len * heads
        ),
        name="attend",
    )(length, keys, values, *blocks)
    return outs[:groups], outs[groups:]


def weight_kernel(place_ref, states_ref, *refs):
    in_refs, own_ref, sib_ref = refs[:-2], refs[-2], refs[-1]
    states = states_ref[...]
    groups = 2
    for e in range(len(in_refs) // groups):
        for a in range(groups):
            piece = lax.dot_general(
                in_refs[e * groups + a][...], states, TN, preferred_element_type=F32
            )
            index = e * groups + a
            away, seq = place_ref[2 * index], place_ref[2 * index + 1]

            @pl.when(away == 0)
            def _(piece=piece, seq=seq):
                own_ref[seq] = piece

            @pl.when(away != 0)
            def _(piece=piece, seq=seq):
                sib_ref[seq] = piece.astype(BF16)


def weight_parts(place, states, blocks, seq_size):
    src_len, width = states.shape
    tall = blocks[0].shape[1]
    shape = (seq_size, tall, width)
    return pl.pallas_call(
        weight_kernel,
        out_shape=[jax.ShapeDtypeStruct(shape, F32), jax.ShapeDtypeStruct(shape, BF16)],
        in_specs=[SMEM_SPEC] + [VMEM_SPEC] * (1 + len(blocks)),
        out_specs=[VMEM_SPEC] * 2,
        compiler_params=pltpu.CompilerParams(vmem_limit_bytes=VMEM_BYTES),
        cost_estimate=cost(2 * len(blocks) * src_len * tall * width, 6 << 20),
        name="weight_parts",
    )(place, states, *blocks)


def state_kernel(chunks, order_ref, w_ref, *refs):
    in_refs, out_ref, total_ref = refs[:-2], refs[-2], refs[-1]
    total_ref[...] = jnp.zeros_like(total_ref)
    per_chunk = len(in_refs) // chunks
    for c in range(chunks):
        at = slice(c * LANES, (c + 1) * LANES)
        for index in range(per_chunk):
            piece = order_ref[index]
            weight = jnp.concatenate([w_ref[piece, 0, at], w_ref[piece, 1, at]], axis=0)
            total_ref[...] += jnp.dot(
                in_refs[c * per_chunk + index][...], weight, preferred_element_type=F32
            )
    out_ref[...] = total_ref[...].astype(BF16)


def state_grads(order, weights, blocks, chunks):
    src_len, width = blocks[0].shape[0], weights.shape[-1]
    return pl.pallas_call(
        functools.partial(state_kernel, chunks),
        out_shape=jax.ShapeDtypeStruct((src_len, width), BF16),
        in_specs=[SMEM_SPEC] + [VMEM_SPEC] * (1 + len(blocks)),
        out_specs=VMEM_SPEC,
        scratch_shapes=[pltpu.VMEM((src_len, width), F32)],
        compiler_params=pltpu.CompilerParams(vmem_limit_bytes=VMEM_BYTES),
        cost_estimate=cost(2 * len(blocks) * src_len * 2 * LANES * width, 8 << 20),
        name="state_grads",
    )(order, weights, *blocks)


def swap(x, axes, size, distance):
    return lax.ppermute(x, axes, [(i, i ^ distance) for i in range(size)])


def exchange(blocks):
    peers = len(blocks)
    far_first = sorted(range(1, peers), key=lambda d: -(d % (peers // 2)))
    got = {d: swap(blocks[d], PEERS, peers, d) for d in far_first}
    return [blocks[0]] + [got[d] for d in range(1, peers)]


def gather_mdl(pair):
    near = [swap(b, "mdl", 4, 1) for b in pair]
    over = [swap(b, "mdl", 4, 2) for b in pair]
    across = [swap(near[0], "mdl", 4, 2), swap(over[1], "mdl", 4, 1)]
    return list(pair) + near + over + across


def scatter_line(own, sib, seq_size):
    place = lax.axis_index("seq")
    got = swap(sib, "grp", 2, 1)

    def piece(index):
        index = jnp.clip(index, 0, seq_size - 1)
        mine = lax.dynamic_index_in_dim(own, index, 0, keepdims=False)
        other = lax.dynamic_index_in_dim(got, index, 0, keepdims=False)
        return mine + other.astype(F32)

    right = left = None
    last = seq_size - 1
    for t in range(last):
        send_right, send_left = piece(last - t + place), piece(t + place - last)
        if t > 0:
            send_right, send_left = send_right + right.astype(F32), send_left + left.astype(F32)
        right = lax.ppermute(
            send_right.astype(BF16), "seq", [(z, z + 1) for z in range(t + 1)]
        )
        left = lax.ppermute(
            send_left.astype(BF16), "seq", [(last - z, last - z - 1) for z in range(t + 1)]
        )
    return piece(place) + right.astype(F32) + left.astype(F32)


def block_grads(query_block, grad_block, key_local, value_local, key_valid):
    score_scale = key_local.shape[-1] ** (-0.5)
    scores = (
        jnp.einsum("rhe,khe->hrk", query_block, key_local, preferred_element_type=jnp.float32)
        * score_scale
    )
    scores = jnp.where(key_valid[None, None, :], scores, -1e30)
    row_peak = jnp.max(scores, axis=-1, keepdims=True)
    exp_terms = jnp.exp(scores - row_peak)
    attn_probs = exp_terms / jnp.sum(exp_terms, axis=-1, keepdims=True)
    probs_b = attn_probs.astype(jnp.bfloat16)
    context = jnp.einsum("hrk,khe->rhe", probs_b, value_local, preferred_element_type=jnp.float32)
    row_delta = jnp.sum(grad_block.astype(jnp.float32) * context, axis=-1)
    prob_grad = jnp.einsum(
        "rhe,khe->hrk", grad_block, value_local, preferred_element_type=jnp.float32
    )
    score_grad = (attn_probs * (prob_grad - row_delta.T[:, :, None]) * score_scale).astype(
        jnp.bfloat16
    )
    query_grad = jnp.einsum(
        "hrk,khe->rhe", score_grad, key_local, preferred_element_type=jnp.float32
    ).astype(jnp.bfloat16)
    key_grad = jnp.einsum(
        "hrk,rhe->khe", score_grad, query_block, preferred_element_type=jnp.float32
    )
    value_grad = jnp.einsum("hrk,rhe->khe", probs_b, grad_block, preferred_element_type=jnp.float32)
    return (query_grad, key_grad, value_grad)


def any_mesh(queries, out_grads, owners, src_keys, src_values, states, kv_weight, src_lengths):
    peer_count = lax.axis_size(("grp", "seq"))
    tgt_dev, tgt_len, inner_dev = queries.shape
    per_peer = max(2, 2 * tgt_dev // peer_count)
    slot_count = peer_count * per_peer
    row_width = tgt_len * inner_dev
    head_dim = HEAD_DIM
    local_heads = inner_dev // head_dim
    src_len = src_keys.shape[1]
    member = (owners[:, None] == jnp.arange(peer_count, dtype=jnp.int32)[None, :]).astype(jnp.int32)
    earlier = jnp.cumsum(member, axis=0) - member
    rank_own = jnp.sum(earlier * member, axis=1)
    slot_of = owners * per_peer + rank_own
    selector = (jnp.arange(slot_count, dtype=jnp.int32)[:, None] == slot_of[None, :]).astype(
        jnp.bfloat16
    )
    send_query = jnp.dot(
        selector, queries.reshape(tgt_dev, row_width), preferred_element_type=jnp.float32
    ).astype(jnp.bfloat16)
    send_grad = jnp.dot(
        selector, out_grads.reshape(tgt_dev, row_width), preferred_element_type=jnp.float32
    ).astype(jnp.bfloat16)
    got_query, got_grad = (
        lax.all_to_all(send_query, ("grp", "seq"), split_axis=0, concat_axis=0, tiled=True),
        lax.all_to_all(send_grad, ("grp", "seq"), split_axis=0, concat_axis=0, tiled=True),
    )
    total_rows = slot_count * tgt_len
    block_rows = 512
    block_count = total_rows // block_rows
    query_rows = got_query.reshape(block_count, block_rows, local_heads, head_dim)
    grad_rows = got_grad.reshape(block_count, block_rows, local_heads, head_dim)
    key_local = src_keys[0].reshape(src_len, local_heads, head_dim)
    value_local = src_values[0].reshape(src_len, local_heads, head_dim)
    key_valid = jnp.arange(src_len, dtype=jnp.int32) < src_lengths[0]

    def attend_step(totals, block_pair):
        query_grad, key_grad, value_grad = block_grads(
            block_pair[0], block_pair[1], key_local, value_local, key_valid
        )
        return ((totals[0] + key_grad, totals[1] + value_grad), query_grad)

    zero_grads = jnp.zeros((src_len, local_heads, head_dim), jnp.float32)
    (key_total, value_total), query_blocks = lax.scan(
        attend_step, (zero_grads, zero_grads), (query_rows, grad_rows)
    )
    back_rows = query_blocks.reshape(slot_count, row_width)
    returned = lax.all_to_all(back_rows, ("grp", "seq"), split_axis=0, concat_axis=0, tiled=True)
    query_out = lax.dot_general(
        selector, returned, (((0,), (0,)), ((), ())), preferred_element_type=jnp.float32
    )
    query_out = query_out.astype(jnp.bfloat16).reshape(tgt_dev, tgt_len, inner_dev)
    key_bf = key_total.reshape(src_len, inner_dev).astype(jnp.bfloat16)
    value_bf = value_total.reshape(src_len, inner_dev).astype(jnp.bfloat16)
    key_all, value_all = (
        lax.all_gather(key_bf, "mdl", axis=1, tiled=True),
        lax.all_gather(value_bf, "mdl", axis=1, tiled=True),
    )
    weight_piece = lax.all_gather(kv_weight, ("grp", "seq"), axis=0, tiled=True)
    key_cols = key_all
    value_cols = value_all
    total = jnp.dot(key_cols, weight_piece[:, 0, :], preferred_element_type=jnp.float32)
    state_sum = total + jnp.dot(
        value_cols, weight_piece[:, 1, :], preferred_element_type=jnp.float32
    )
    state_out = state_sum.astype(jnp.bfloat16).reshape(1, src_len, kv_weight.shape[2])
    flat_states = states.reshape(src_len, states.shape[2])
    key_cols = key_all
    value_cols = value_all
    grad_key = lax.dot_general(
        key_cols, flat_states, (((0,), (0,)), ((), ())), preferred_element_type=jnp.float32
    )
    grad_value = lax.dot_general(
        value_cols, flat_states, (((0,), (0,)), ((), ())), preferred_element_type=jnp.float32
    )
    weight_out = lax.psum_scatter(
        jnp.stack([grad_key, grad_value], axis=1), ("grp", "seq"), scatter_dimension=0, tiled=True
    )
    return (query_out, state_out, weight_out)


def on_device(queries, out_grads, owners, src_keys, src_values, states, kv_weight, src_lengths):
    seq_size = lax.axis_size("seq")
    peers = lax.axis_size(PEERS)
    targets, rows, width = queries.shape
    per_peer = max(2, 2 * targets // peers)
    src_len = src_keys.shape[1]
    chunks = 2
    groups = width // (chunks * LANES)
    me = lax.axis_index(PEERS).astype(jnp.int32)
    mdl = lax.axis_index("mdl").astype(jnp.int32)
    grp = lax.axis_index("grp").astype(jnp.int32)
    table, sends = pack(me[None], owners, queries, out_grads, peers, per_peer, chunks)
    keys, values = src_keys[0], src_values[0]
    flat_states = states[0]
    tall = jnp.transpose(kv_weight, (1, 0, 2))

    source = mdl ^ (jnp.arange(4 * groups, dtype=jnp.int32) // groups)
    order = source * groups + jnp.arange(4 * groups, dtype=jnp.int32) % groups
    place = jnp.stack([(order // seq_size) ^ grp, order % seq_size], axis=1).reshape(-1)

    got = [exchange(sends[c]) for c in range(chunks)]
    gathered, back, sums = [], [], []
    for c in range(chunks):
        pair, query_blocks = attend(src_lengths, keys, values, got[c], c, chunks)
        back.append(query_blocks)
        gathered.append(gather_mdl(pair))
    tall, _ = lax.optimization_barrier((tall, got[1][1]))
    weights = lax.all_gather(tall, PEERS, axis=0)
    for c in range(chunks):
        own, sib = weight_parts(place, flat_states, gathered[c], seq_size)
        sums.append(scatter_line(own, sib, seq_size))
    returned = [exchange(b) for b in back]
    state_out = state_grads(order, weights, [b for part in gathered for b in part], chunks)
    query_out = unpack(table, returned, targets, rows, width, peers, per_peer)
    weight_out = jnp.concatenate(
        [s.reshape(2, LANES, width).transpose(1, 0, 2) for s in sums], axis=0
    )
    return (query_out, state_out.reshape(1, src_len, width), weight_out)


def solution(mesh):
    spec = P(PEERS, None, "mdl")
    in_specs = (spec, spec, P(PEERS), spec, spec, spec, spec, P(PEERS))
    tuned = (mesh.shape["grp"], mesh.shape["seq"], mesh.shape["mdl"]) == (2, 4, 4)
    return jax.shard_map(
        on_device if tuned else any_mesh, mesh=mesh, in_specs=in_specs, out_specs=(spec, spec, spec), check_vma=False
    )
```

```python
import functools

import jax
import jax.numpy as jnp
from jax import lax
from jax.experimental import pallas as pl
from jax.experimental.pallas import tpu as pltpu
from jax.sharding import PartitionSpec as P

HEAD_DIM = 64
CHUNKS = 2
LANES = 128
PEERS = ("grp", "seq")
BF16 = jnp.bfloat16
F32 = jnp.float32
VMEM_BYTES = 16 * 1024 * 1024
ATTEND_BYTES = 24 * 1024 * 1024

VMEM_SPEC = pl.BlockSpec(memory_space=pltpu.VMEM)
ANY_SPEC = pl.BlockSpec(memory_space=pl.ANY)
SMEM_SPEC = pl.BlockSpec(memory_space=pltpu.SMEM)
NT = (((1,), (1,)), ((), ()))
TN = (((0,), (0,)), ((), ()))


def cost(flops, bytes_accessed, transcendentals=0):
    return pl.CostEstimate(
        flops=flops, bytes_accessed=bytes_accessed, transcendentals=transcendentals
    )


def fetch(sources, targets, sems):
    copies = []
    for i, (source, target) in enumerate(zip(sources, targets)):
        copies.append(pltpu.make_async_copy(source, target, sems.at[i]))
        copies[-1].start()
    return copies


def pack_kernel(peers, per_peer, chunk, chunks, me_ref, owners_hbm, q_hbm, g_hbm, *refs):
    both_ref, count_ref, owners_ref, q_ref, g_ref, sems = refs[-6:]
    table_ref, out_refs = refs[-8 - peers // 2], refs[-7 - peers // 2 : -6]
    targets, rows, width = q_ref.shape
    groups = width // (chunks * LANES)
    copies = fetch([owners_hbm, q_hbm, g_hbm], [owners_ref, q_ref, g_ref], sems)
    both_ref[targets] = jnp.zeros(both_ref.shape[1:], BF16)
    me = me_ref[0]

    def clear_count(i, _):
        count_ref[i] = 0
        return 0

    def clear_slot(i, _):
        table_ref[i] = targets
        return 0

    def place(t, _):
        distance = owners_ref[t] ^ me
        rank = count_ref[distance]
        table_ref[distance * per_peer + rank] = t
        count_ref[distance] = rank + 1
        return 0

    lax.fori_loop(0, peers, clear_count, 0)
    lax.fori_loop(0, peers * per_peer, clear_slot, 0, unroll=8)
    copies[0].wait()
    lax.fori_loop(0, targets, place, 0, unroll=8)
    copies[1].wait()
    copies[2].wait()
    for a in range(groups):
        lane = (a * chunks + chunk) * LANES
        both = jnp.concatenate(
            [
                q_ref[:, :, lane : lane + LANES].astype(F32),
                g_ref[:, :, lane : lane + LANES].astype(F32),
            ],
            axis=1,
        )
        both_ref[:targets, :, a * LANES : (a + 1) * LANES] = both.astype(BF16)
    half = peers // 2
    for d in range(half):

        def move(slot, _, d=d):
            out_refs[d][slot] = both_ref[table_ref[d * per_peer + slot]]
            out_refs[half][d, slot] = both_ref[table_ref[(half + d) * per_peer + slot]]
            return 0

        lax.fori_loop(0, per_peer, move, 0, unroll=4)


def pack(me, owners, queries, out_grads, peers, per_peer, chunk, chunks):
    targets, rows, width = queries.shape
    part, half = width // chunks, peers // 2
    block = (per_peer, 2 * rows, part)
    outs = pl.pallas_call(
        functools.partial(pack_kernel, peers, per_peer, chunk, chunks),
        out_shape=[jax.ShapeDtypeStruct((peers * per_peer,), jnp.int32)]
        + [jax.ShapeDtypeStruct(block, BF16)] * half
        + [jax.ShapeDtypeStruct((half,) + block, BF16)],
        in_specs=[SMEM_SPEC, ANY_SPEC, ANY_SPEC, ANY_SPEC],
        out_specs=[SMEM_SPEC] + [VMEM_SPEC] * (half + 1),
        scratch_shapes=[
            pltpu.VMEM((targets + 1, 2 * rows, part), BF16),
            pltpu.SMEM((peers,), jnp.int32),
            pltpu.SMEM((targets,), jnp.int32),
            pltpu.VMEM(queries.shape, BF16),
            pltpu.VMEM(queries.shape, BF16),
            pltpu.SemaphoreType.DMA((3,)),
        ],
        compiler_params=pltpu.CompilerParams(vmem_limit_bytes=VMEM_BYTES),
        cost_estimate=cost(0, 3 << 20),
        name="pack_targets",
    )(me, owners, queries, out_grads)
    return outs[0], outs[1:-1], outs[-1]


def hold_kernel(count, *refs):
    for x_ref, out_ref in zip(refs[:count], refs[-count:]):
        out_ref[...] = x_ref[...]


def hold(arrays, earlier):
    return pl.pallas_call(
        functools.partial(hold_kernel, len(arrays)),
        out_shape=[jax.ShapeDtypeStruct(x.shape, x.dtype) for x in arrays],
        in_specs=[VMEM_SPEC] * (len(arrays) + len(earlier)),
        out_specs=[VMEM_SPEC] * len(arrays),
        compiler_params=pltpu.CompilerParams(vmem_limit_bytes=VMEM_BYTES),
        cost_estimate=cost(0, 1 << 20),
        name="hold",
    )(*arrays, *earlier)


def merge_kernel(half, *refs):
    blocks, got_ref, out_refs = refs[:half], refs[half], refs[-half:]
    for d in range(half):
        out_refs[d][0] = blocks[d][...]
        out_refs[d][1] = got_ref[d]


def merge(blocks, got, earlier):
    half = len(blocks)
    return pl.pallas_call(
        functools.partial(merge_kernel, half),
        out_shape=[jax.ShapeDtypeStruct((2,) + blocks[0].shape, BF16)] * half,
        in_specs=[VMEM_SPEC] * (half + 1 + len(earlier)),
        out_specs=[VMEM_SPEC] * half,
        compiler_params=pltpu.CompilerParams(vmem_limit_bytes=VMEM_BYTES),
        cost_estimate=cost(0, 1 << 20),
        name="merge",
    )(*blocks, got, *earlier)


def unpack_kernel(peers, per_peer, table_ref, *refs):
    half = peers // 2
    near_refs, over_ref, out_ref = refs[:half], refs[half], refs[half + 1]
    near_s, over_s, rows_ref, sems = refs[half + 2 :]
    targets, rows, width = out_ref.shape
    block_rows = per_peer * rows
    copies = fetch(
        list(near_refs) + [over_ref], [near_s.at[d] for d in range(half)] + [over_s], sems
    )
    for copy in copies:
        copy.wait()
    for d in range(peers):
        block = near_s[d, :block_rows] if d < half else over_s[d - half]
        rows_ref[d * per_peer : (d + 1) * per_peer] = block.astype(F32).reshape(
            per_peer, rows, width
        )

    def move(slot, _):
        t = table_ref[slot]

        @pl.when(t < targets)
        def _():
            out_ref[t] = rows_ref[slot].astype(BF16)

        return 0

    lax.fori_loop(0, peers * per_peer, move, 0)


def unpack(table, near, over, targets, rows, per_peer):
    half, width = len(near), near[0].shape[1]
    return pl.pallas_call(
        functools.partial(unpack_kernel, 2 * half, per_peer),
        out_shape=jax.ShapeDtypeStruct((targets, rows, width), BF16),
        in_specs=[SMEM_SPEC] + [ANY_SPEC] * (half + 1),
        out_specs=VMEM_SPEC,
        scratch_shapes=[
            pltpu.VMEM((half,) + near[0].shape, BF16),
            pltpu.VMEM(over.shape, BF16),
            pltpu.VMEM((2 * half * per_peer, rows, width), F32),
            pltpu.SemaphoreType.DMA((half + 1,)),
        ],
        compiler_params=pltpu.CompilerParams(vmem_limit_bytes=VMEM_BYTES),
        cost_estimate=cost(0, 3 << 20),
        name="unpack_query_grads",
    )(table, *near, over)


def attend_kernel(peers, chunk, chunks, waits, len_ref, k_ref, v_ref, *refs):
    half = peers // 2
    in_refs, before_refs = refs[:half], refs[half : half + chunk]
    groups = k_ref.shape[1] // (chunks * LANES)
    outs = refs[half + chunk + waits : -6]
    kv_ref, out_refs = outs[0], outs[1:]
    q_s, g_s, o_s, kt_s, kg_s, vg_s = refs[-6:]
    src_len = k_ref.shape[0]
    _, per_peer, double, width = in_refs[0].shape
    rows = double // 2
    block_rows = per_peer * rows
    total_rows = peers * block_rows
    tile = min(256, total_rows)
    scale = HEAD_DIM**-0.5
    for d in range(peers):
        both = in_refs[d // 2][d % 2].astype(F32)
        at = slice(d * block_rows, (d + 1) * block_rows)
        q_s[at] = (both[:, :rows] * scale).reshape(block_rows, width).astype(BF16)
        g_s[at] = both[:, rows:].reshape(block_rows, width).astype(BF16)
    valid = lax.broadcasted_iota(jnp.int32, (src_len, 1), 0) < len_ref[0]
    lane_head = lax.broadcasted_iota(jnp.int32, (1, LANES), 1) // HEAD_DIM
    for a in range(groups):
        lane = (a * chunks + chunk) * LANES
        mine = slice(a * LANES, (a + 1) * LANES)
        kt_s[...] = (k_ref[:, lane : lane + LANES].astype(F32) * scale).T.astype(BF16)
        kg_s[...] = jnp.zeros_like(kg_s)
        vg_s[...] = jnp.zeros_like(vg_s)

        def step(i, _, lane=lane, mine=mine):
            at = pl.ds(pl.multiple_of(i * tile, tile), tile)
            q_pair, g_pair = q_s[at, mine], g_s[at, mine]
            k_pair, v_pair = k_ref[:, lane : lane + LANES], v_ref[:, lane : lane + LANES]
            parts = []
            for h in range(LANES // HEAD_DIM):
                q_h = jnp.where(lane_head == h, q_pair, jnp.zeros_like(q_pair))
                g_h = jnp.where(lane_head == h, g_pair, jnp.zeros_like(g_pair))
                scores = lax.dot_general(k_pair, q_h, NT, preferred_element_type=F32)
                scores = jnp.where(valid, scores, -1e30)
                prob_grad = lax.dot_general(v_pair, g_h, NT, preferred_element_type=F32)
                peak = jnp.max(scores, axis=0, keepdims=True)
                terms = jnp.exp(scores - peak)
                probs = terms * (1.0 / jnp.sum(terms, axis=0, keepdims=True))
                row_delta = jnp.sum(probs * prob_grad, axis=0, keepdims=True)
                score_grad = (probs * (prob_grad - row_delta)).astype(BF16)
                vg_s[...] += jnp.dot(probs.astype(BF16), g_h, preferred_element_type=F32)
                kg_s[...] += jnp.dot(score_grad, q_h, preferred_element_type=F32)
                parts.append(
                    jnp.dot(
                        kt_s[h * HEAD_DIM : (h + 1) * HEAD_DIM],
                        score_grad,
                        preferred_element_type=F32,
                    )
                )
            o_s[at, mine] = jnp.concatenate(parts, axis=0).T.astype(BF16)
            return 0

        lax.fori_loop(0, total_rows // tile, step, 0)
        kv_ref[a, :, :LANES] = kg_s[...].astype(BF16)
        kv_ref[a, :, LANES:] = vg_s[...].astype(BF16)
    if chunk < chunks - 1:
        out_refs[0][...] = o_s[...]
        return
    for d in range(half):
        at = slice(2 * d * block_rows, 2 * (d + 1) * block_rows)
        for c, part_ref in enumerate((*before_refs, o_s)):
            for a in range(groups):
                lane = (a * chunks + c) * LANES
                out_refs[d][:, lane : lane + LANES] = part_ref[at, a * LANES : (a + 1) * LANES]


def attend(length, keys, values, blocks, before, earlier):
    chunk, chunks = len(before), CHUNKS
    half = len(blocks)
    peers = 2 * half
    src_len, width = keys.shape
    _, per_peer, double, part = blocks[0].shape
    block_rows = per_peer * double // 2
    total_rows = peers * block_rows
    groups = part // LANES
    heads = part // HEAD_DIM
    query_shapes = [jax.ShapeDtypeStruct((total_rows, part), BF16)]
    if chunk == chunks - 1:
        query_shapes = [jax.ShapeDtypeStruct((2 * block_rows, width), BF16)] * half
    outs = pl.pallas_call(
        functools.partial(attend_kernel, peers, chunk, chunks, len(earlier)),
        out_shape=[jax.ShapeDtypeStruct((groups, src_len, 2 * LANES), BF16)] + query_shapes,
        in_specs=[SMEM_SPEC] + [VMEM_SPEC] * (2 + half + chunk + len(earlier)),
        out_specs=[VMEM_SPEC] * (1 + len(query_shapes)),
        scratch_shapes=[
            pltpu.VMEM((total_rows, part), BF16),
            pltpu.VMEM((total_rows, part), BF16),
            pltpu.VMEM((total_rows, part), BF16),
            pltpu.VMEM((LANES, src_len), BF16),
            pltpu.VMEM((src_len, LANES), F32),
            pltpu.VMEM((src_len, LANES), F32),
        ],
        compiler_params=pltpu.CompilerParams(vmem_limit_bytes=ATTEND_BYTES),
        cost_estimate=cost(
            40 * total_rows * src_len * HEAD_DIM * heads, 4 << 20, total_rows * src_len * heads
        ),
        name="attend",
    )(length, keys, values, *blocks, *before, *earlier)
    return outs[0], outs[1:]


def weight_kernel(blocks, place_ref, states_ref, *refs):
    own_ref, sib_ref, states_s, pairs_s, across_s, sems = refs[-6:]
    targets = [states_s] + [pairs_s.at[e] for e in range(3)] + [across_s.at[a] for a in range(2)]
    copies = fetch([states_ref] + list(refs[:blocks]), targets, sems)
    copies[0].wait()
    states = states_s[...]
    for index in range(8):
        e, a = index // 2, index % 2
        if e < 3 and a == 0:
            copies[1 + e].wait()
        elif e == 3:
            copies[4 + a].wait()
        block = pairs_s[e, a] if e < 3 else across_s[a]
        piece = lax.dot_general(block, states, TN, preferred_element_type=F32)
        away, seq = place_ref[2 * index], place_ref[2 * index + 1]

        @pl.when(away == 0)
        def _(piece=piece, seq=seq):
            own_ref[seq] = piece

        @pl.when(away != 0)
        def _(piece=piece, seq=seq):
            sib_ref[seq] = piece.astype(BF16)


def weight_parts(place, states, blocks, seq_size, earlier):
    src_len, width = states.shape
    tall = blocks[0].shape[2]
    shape = (seq_size, tall, width)
    return pl.pallas_call(
        functools.partial(weight_kernel, len(blocks)),
        out_shape=[jax.ShapeDtypeStruct(shape, F32), jax.ShapeDtypeStruct(shape, BF16)],
        in_specs=[SMEM_SPEC] + [ANY_SPEC] * (1 + len(blocks) + len(earlier)),
        out_specs=[VMEM_SPEC] * 2,
        scratch_shapes=[
            pltpu.VMEM((src_len, width), BF16),
            pltpu.VMEM((3, 2, src_len, tall), BF16),
            pltpu.VMEM((2, src_len, tall), BF16),
            pltpu.SemaphoreType.DMA((1 + len(blocks),)),
        ],
        compiler_params=pltpu.CompilerParams(vmem_limit_bytes=VMEM_BYTES),
        cost_estimate=cost(16 * src_len * tall * width, 6 << 20),
        name="weight_parts",
    )(place, states, *blocks, *earlier)


def combine_kernel(chunks, seq_ref, *refs):
    parts, outs = refs[: 2 * chunks], refs[2 * chunks :]
    for d in range(len(outs)):
        index = seq_ref[0] ^ d
        for c in range(chunks):
            total = parts[2 * c][index] + parts[2 * c + 1][index].astype(F32)
            outs[d][c] = total.astype(outs[d].dtype)


def combine(seq, parts):
    pieces, tall, width = parts[0][0].shape
    shape = (len(parts), tall, width)
    return pl.pallas_call(
        functools.partial(combine_kernel, len(parts)),
        out_shape=[jax.ShapeDtypeStruct(shape, F32)]
        + [jax.ShapeDtypeStruct(shape, BF16)] * (pieces - 1),
        in_specs=[SMEM_SPEC] + [VMEM_SPEC] * (2 * len(parts)),
        out_specs=[VMEM_SPEC] * pieces,
        compiler_params=pltpu.CompilerParams(vmem_limit_bytes=VMEM_BYTES),
        cost_estimate=cost(0, 6 << 20),
        name="combine",
    )(seq, *[x for part in parts for x in part])


def state_kernel(chunks, order_ref, w_ref, *refs):
    in_refs, out_ref = refs[: 5 * chunks], refs[5 * chunks]
    total_ref, w_s, pairs_s, across_s, sems = refs[5 * chunks + 1 :]
    targets = []
    for c in range(chunks):
        targets += [pairs_s.at[c, e] for e in range(3)] + [across_s.at[c, a] for a in range(2)]
    copies = fetch([w_ref] + list(in_refs), [w_s] + targets, sems)
    for copy in copies:
        copy.wait()
    total_ref[...] = jnp.zeros_like(total_ref)
    for c in range(chunks):
        at = slice(c * LANES, (c + 1) * LANES)
        for index in range(8):
            e, a = index // 2, index % 2
            piece = order_ref[index]
            weight = jnp.concatenate([w_s[piece, 0, at], w_s[piece, 1, at]], axis=0)
            block = pairs_s[c, e, a] if e < 3 else across_s[c, a]
            total_ref[...] += jnp.dot(block, weight, preferred_element_type=F32)
    out_ref[...] = total_ref[...].astype(BF16)


def state_grads(order, weights, blocks, chunks):
    src_len, tall = blocks[0].shape[1:]
    width = weights.shape[-1]
    return pl.pallas_call(
        functools.partial(state_kernel, chunks),
        out_shape=jax.ShapeDtypeStruct((src_len, width), BF16),
        in_specs=[SMEM_SPEC] + [ANY_SPEC] * (1 + len(blocks)),
        out_specs=VMEM_SPEC,
        scratch_shapes=[
            pltpu.VMEM((src_len, width), F32),
            pltpu.VMEM(weights.shape, BF16),
            pltpu.VMEM((chunks, 3, 2, src_len, tall), BF16),
            pltpu.VMEM((chunks, 2, src_len, tall), BF16),
            pltpu.SemaphoreType.DMA((1 + len(blocks),)),
        ],
        compiler_params=pltpu.CompilerParams(vmem_limit_bytes=ATTEND_BYTES),
        cost_estimate=cost(32 * src_len * 2 * LANES * width, 8 << 20),
        name="state_grads",
    )(order, weights, *blocks)


def swap(x, axes, size, distance):
    return lax.ppermute(x, axes, [(i, i ^ distance) for i in range(size)])


def ring(x):
    size = lax.axis_size("seq")
    return lax.ppermute(x, "seq", [(z, (z + 1) % size) for z in range(size)])


def exchange(blocks, sib, earlier):
    half = len(blocks)
    got = swap(sib, "grp", 2, 1)
    pairs = merge(blocks, got, earlier)
    line = {d: swap(pairs[d], "seq", half, d) for d in range(half - 1, 0, -1)}
    return [pairs[0]] + [line[d] for d in range(1, half)], pairs[1:]


def send_back(pairs):
    half, rows = len(pairs), pairs[0].shape[0] // 2
    line = {d: swap(pairs[d], "seq", half, d) for d in range(half - 1, 0, -1)}
    near = [pairs[0]] + [line[d] for d in range(1, half)]
    return near, swap(jnp.stack([pair[rows:] for pair in near]), "grp", 2, 1)


def gather_near(pair):
    return [pair, swap(pair, "mdl", 4, 1), swap(pair, "mdl", 4, 2)]


def gather_across(pair, near, over, earlier=()):
    first, second = near[0], over[1]
    if earlier:
        first, second = hold([first, second], earlier)
    return [pair, near, over, swap(first, "mdl", 4, 2), swap(second, "mdl", 4, 1)]


def block_grads(query_block, grad_block, key_local, value_local, key_valid):
    score_scale = key_local.shape[-1] ** (-0.5)
    scores = (
        jnp.einsum("rhe,khe->hrk", query_block, key_local, preferred_element_type=jnp.float32)
        * score_scale
    )
    scores = jnp.where(key_valid[None, None, :], scores, -1e30)
    row_peak = jnp.max(scores, axis=-1, keepdims=True)
    exp_terms = jnp.exp(scores - row_peak)
    attn_probs = exp_terms / jnp.sum(exp_terms, axis=-1, keepdims=True)
    probs_b = attn_probs.astype(jnp.bfloat16)
    context = jnp.einsum("hrk,khe->rhe", probs_b, value_local, preferred_element_type=jnp.float32)
    row_delta = jnp.sum(grad_block.astype(jnp.float32) * context, axis=-1)
    prob_grad = jnp.einsum(
        "rhe,khe->hrk", grad_block, value_local, preferred_element_type=jnp.float32
    )
    score_grad = (attn_probs * (prob_grad - row_delta.T[:, :, None]) * score_scale).astype(
        jnp.bfloat16
    )
    query_grad = jnp.einsum(
        "hrk,khe->rhe", score_grad, key_local, preferred_element_type=jnp.float32
    ).astype(jnp.bfloat16)
    key_grad = jnp.einsum(
        "hrk,rhe->khe", score_grad, query_block, preferred_element_type=jnp.float32
    )
    value_grad = jnp.einsum("hrk,rhe->khe", probs_b, grad_block, preferred_element_type=jnp.float32)
    return (query_grad, key_grad, value_grad)


def any_mesh(queries, out_grads, owners, src_keys, src_values, states, kv_weight, src_lengths):
    peer_count = lax.axis_size(("grp", "seq"))
    tgt_dev, tgt_len, inner_dev = queries.shape
    per_peer = max(2, 2 * tgt_dev // peer_count)
    slot_count = peer_count * per_peer
    row_width = tgt_len * inner_dev
    head_dim = HEAD_DIM
    local_heads = inner_dev // head_dim
    src_len = src_keys.shape[1]
    member = (owners[:, None] == jnp.arange(peer_count, dtype=jnp.int32)[None, :]).astype(jnp.int32)
    earlier = jnp.cumsum(member, axis=0) - member
    rank_own = jnp.sum(earlier * member, axis=1)
    slot_of = owners * per_peer + rank_own
    selector = (jnp.arange(slot_count, dtype=jnp.int32)[:, None] == slot_of[None, :]).astype(
        jnp.bfloat16
    )
    send_query = jnp.dot(
        selector, queries.reshape(tgt_dev, row_width), preferred_element_type=jnp.float32
    ).astype(jnp.bfloat16)
    send_grad = jnp.dot(
        selector, out_grads.reshape(tgt_dev, row_width), preferred_element_type=jnp.float32
    ).astype(jnp.bfloat16)
    got_query, got_grad = (
        lax.all_to_all(send_query, ("grp", "seq"), split_axis=0, concat_axis=0, tiled=True),
        lax.all_to_all(send_grad, ("grp", "seq"), split_axis=0, concat_axis=0, tiled=True),
    )
    total_rows = slot_count * tgt_len
    block_rows = 512
    block_count = total_rows // block_rows
    query_rows = got_query.reshape(block_count, block_rows, local_heads, head_dim)
    grad_rows = got_grad.reshape(block_count, block_rows, local_heads, head_dim)
    key_local = src_keys[0].reshape(src_len, local_heads, head_dim)
    value_local = src_values[0].reshape(src_len, local_heads, head_dim)
    key_valid = jnp.arange(src_len, dtype=jnp.int32) < src_lengths[0]

    def attend_step(totals, block_pair):
        query_grad, key_grad, value_grad = block_grads(
            block_pair[0], block_pair[1], key_local, value_local, key_valid
        )
        return ((totals[0] + key_grad, totals[1] + value_grad), query_grad)

    zero_grads = jnp.zeros((src_len, local_heads, head_dim), jnp.float32)
    (key_total, value_total), query_blocks = lax.scan(
        attend_step, (zero_grads, zero_grads), (query_rows, grad_rows)
    )
    back_rows = query_blocks.reshape(slot_count, row_width)
    returned = lax.all_to_all(back_rows, ("grp", "seq"), split_axis=0, concat_axis=0, tiled=True)
    query_out = lax.dot_general(
        selector, returned, (((0,), (0,)), ((), ())), preferred_element_type=jnp.float32
    )
    query_out = query_out.astype(jnp.bfloat16).reshape(tgt_dev, tgt_len, inner_dev)
    key_bf = key_total.reshape(src_len, inner_dev).astype(jnp.bfloat16)
    value_bf = value_total.reshape(src_len, inner_dev).astype(jnp.bfloat16)
    key_all, value_all = (
        lax.all_gather(key_bf, "mdl", axis=1, tiled=True),
        lax.all_gather(value_bf, "mdl", axis=1, tiled=True),
    )
    weight_piece = lax.all_gather(kv_weight, ("grp", "seq"), axis=0, tiled=True)
    key_cols = key_all
    value_cols = value_all
    total = jnp.dot(key_cols, weight_piece[:, 0, :], preferred_element_type=jnp.float32)
    state_sum = total + jnp.dot(
        value_cols, weight_piece[:, 1, :], preferred_element_type=jnp.float32
    )
    state_out = state_sum.astype(jnp.bfloat16).reshape(1, src_len, kv_weight.shape[2])
    flat_states = states.reshape(src_len, states.shape[2])
    key_cols = key_all
    value_cols = value_all
    grad_key = lax.dot_general(
        key_cols, flat_states, (((0,), (0,)), ((), ())), preferred_element_type=jnp.float32
    )
    grad_value = lax.dot_general(
        value_cols, flat_states, (((0,), (0,)), ((), ())), preferred_element_type=jnp.float32
    )
    weight_out = lax.psum_scatter(
        jnp.stack([grad_key, grad_value], axis=1), ("grp", "seq"), scatter_dimension=0, tiled=True
    )
    return (query_out, state_out, weight_out)


def on_device(queries, out_grads, owners, src_keys, src_values, states, kv_weight, src_lengths):
    seq_size = lax.axis_size("seq")
    peers = lax.axis_size(PEERS)
    targets, rows, width = queries.shape
    per_peer = max(2, 2 * targets // peers)
    src_len = src_keys.shape[1]
    chunks = CHUNKS
    groups = width // (chunks * LANES)
    me = lax.axis_index(PEERS).astype(jnp.int32)
    mdl = lax.axis_index("mdl").astype(jnp.int32)
    grp = lax.axis_index("grp").astype(jnp.int32)
    keys, values = src_keys[0], src_values[0]
    flat_states = states[0]
    source = mdl ^ (jnp.arange(4 * groups, dtype=jnp.int32) // groups)
    order = source * groups + jnp.arange(4 * groups, dtype=jnp.int32) % groups
    seq = lax.axis_index("seq").astype(jnp.int32)
    distance = (seq - jnp.arange(seq_size, dtype=jnp.int32)) % seq_size
    place = jnp.stack([(order // seq_size) ^ grp, order % seq_size], axis=1).reshape(-1)

    lines = [kv_weight, ring(kv_weight)]
    got, earlier = [], lines[1:]
    for c in range(chunks):
        table, blocks, sib = pack(
            me[None], owners, queries, out_grads, peers, per_peer, c, chunks
        )
        arrived, sent = exchange(blocks, sib, earlier)
        got.append(arrived)
        earlier = arrived[1:]
    gathered, before = [], []
    for c in range(chunks):
        last = c == chunks - 1
        pair, query_blocks = attend(
            src_lengths, keys, values, got[c], before, [pair] if last else sent
        )
        if last:
            pair = hold([pair], gathered[0][1:] + lines[2:])[0]
        else:
            pair, held = hold([pair, lines[1]], got[c + 1][1:])
            lines.append(ring(held))
        before = before + list(query_blocks[:1])
        gathered.append(gather_near(pair))
    lines.append(ring(hold(lines[2:], [pair])[0]))
    gathered = [gather_across(*part, [pair] if c == 0 else []) for c, part in enumerate(gathered)]
    query_blocks = [query_blocks[0], *hold(query_blocks[1:], gathered[0][3:])]
    near, over = send_back(query_blocks)
    sums = []
    for c in range(chunks):
        own, sib = weight_parts(
            place, flat_states, gathered[c], seq_size, near[1:] + sends if c else [pair]
        )
        keep, *sends = combine(seq[None], [(own, swap(sib, "grp", 2, 1))])
        line = [swap(x, "seq", seq_size, d + 1) for d, x in enumerate(sends)]
        sums.append(keep + sum(x.astype(F32) for x in line))
    lines = lines + [swap(x, "grp", 2, 1) for x in lines]
    weights = jnp.stack(lines).transpose(0, 2, 1, 3)
    own_pieces, other_pieces = grp * seq_size + distance, (1 - grp) * seq_size + distance
    piece_at = jnp.zeros((peers,), jnp.int32)
    piece_at = piece_at.at[own_pieces].set(jnp.arange(seq_size, dtype=jnp.int32))
    piece_at = piece_at.at[other_pieces].set(seq_size + jnp.arange(seq_size, dtype=jnp.int32))
    state_out = state_grads(piece_at[order], weights, [b for part in gathered for b in part], chunks)
    query_out = unpack(table, near, over, targets, rows, per_peer)
    weight_sum = jnp.concatenate(sums, axis=0)
    weight_out = weight_sum.reshape(chunks, 2, LANES, width).transpose(0, 2, 1, 3)
    weight_out = weight_out.reshape(chunks * LANES, 2, width)
    return (query_out, state_out.reshape(1, src_len, width), weight_out)


def solution(mesh):
    spec = P(PEERS, None, "mdl")
    in_specs = (spec, spec, P(PEERS), spec, spec, spec, spec, P(PEERS))
    tuned = (mesh.shape["grp"], mesh.shape["seq"], mesh.shape["mdl"]) == (2, 4, 4)
    return jax.shard_map(
        on_device if tuned else any_mesh, mesh=mesh, in_specs=in_specs, out_specs=(spec, spec, spec), check_vma=False
    )
```

```python
import functools

import jax
import jax.numpy as jnp
from jax import lax
from jax.experimental import pallas as pl
from jax.experimental.pallas import tpu as pltpu
from jax.sharding import PartitionSpec as P

HEAD_DIM = 64
CHUNKS = 2
LANES = 128
PEERS = ("grp", "seq")
BF16 = jnp.bfloat16
F32 = jnp.float32
VMEM_BYTES = 16 * 1024 * 1024
ATTEND_BYTES = 24 * 1024 * 1024

VMEM_SPEC = pl.BlockSpec(memory_space=pltpu.VMEM)
HBM_SPEC = pl.BlockSpec(memory_space=pltpu.HBM)
ANY_SPEC = pl.BlockSpec(memory_space=pl.ANY)
SMEM_SPEC = pl.BlockSpec(memory_space=pltpu.SMEM)
NT = (((1,), (1,)), ((), ()))
TN = (((0,), (0,)), ((), ()))


def cost(flops, bytes_accessed, transcendentals=0):
    return pl.CostEstimate(
        flops=flops, bytes_accessed=bytes_accessed, transcendentals=transcendentals
    )


def fetch(sources, targets, sems):
    copies = []
    for i, (source, target) in enumerate(zip(sources, targets)):
        copies.append(pltpu.make_async_copy(source, target, sems.at[i]))
        copies[-1].start()
    return copies


def pack_kernel(peers, per_peer, chunk, chunks, me_ref, owners_hbm, q_hbm, g_hbm, *refs):
    both_ref, count_ref, owners_ref, q_ref, g_ref, sems = refs[-6:]
    table_ref, out_refs = refs[-7 - peers], refs[-6 - peers : -6]
    targets, rows, width = q_ref.shape
    groups = width // (chunks * LANES)
    copies = fetch([owners_hbm, q_hbm, g_hbm], [owners_ref, q_ref, g_ref], sems)
    both_ref[targets] = jnp.zeros(both_ref.shape[1:], BF16)
    me = me_ref[0]

    def clear_count(i, _):
        count_ref[i] = 0
        return 0

    def clear_slot(i, _):
        table_ref[i] = targets
        return 0

    def place(t, _):
        distance = owners_ref[t] ^ me
        rank = count_ref[distance]
        table_ref[distance * per_peer + rank] = t
        count_ref[distance] = rank + 1
        return 0

    lax.fori_loop(0, peers, clear_count, 0)
    lax.fori_loop(0, peers * per_peer, clear_slot, 0, unroll=8)
    copies[0].wait()
    lax.fori_loop(0, targets, place, 0, unroll=8)
    copies[1].wait()
    copies[2].wait()
    for a in range(groups):
        lane = (a * chunks + chunk) * LANES
        both = jnp.concatenate(
            [
                q_ref[:, :, lane : lane + LANES].astype(F32),
                g_ref[:, :, lane : lane + LANES].astype(F32),
            ],
            axis=1,
        )
        both_ref[:targets, :, a * LANES : (a + 1) * LANES] = both.astype(BF16)
    half = peers // 2
    for d in range(half):

        def move(slot, _, d=d):
            out_refs[d][slot] = both_ref[table_ref[d * per_peer + slot]]
            out_refs[half + d][slot] = both_ref[table_ref[(half + d) * per_peer + slot]]
            return 0

        lax.fori_loop(0, per_peer, move, 0, unroll=4)


def pack(me, owners, queries, out_grads, peers, per_peer, chunk, chunks):
    targets, rows, width = queries.shape
    part, half = width // chunks, peers // 2
    block = (per_peer, 2 * rows, part)
    outs = pl.pallas_call(
        functools.partial(pack_kernel, peers, per_peer, chunk, chunks),
        out_shape=[jax.ShapeDtypeStruct((peers * per_peer,), jnp.int32)]
        + [jax.ShapeDtypeStruct(block, BF16)] * peers,
        in_specs=[SMEM_SPEC, HBM_SPEC, HBM_SPEC, HBM_SPEC],
        out_specs=[SMEM_SPEC] + [VMEM_SPEC] * peers,
        scratch_shapes=[
            pltpu.VMEM((targets + 1, 2 * rows, part), BF16),
            pltpu.SMEM((peers,), jnp.int32),
            pltpu.SMEM((targets,), jnp.int32),
            pltpu.VMEM(queries.shape, BF16),
            pltpu.VMEM(queries.shape, BF16),
            pltpu.SemaphoreType.DMA((3,)),
        ],
        compiler_params=pltpu.CompilerParams(vmem_limit_bytes=VMEM_BYTES),
        cost_estimate=cost(0, 3 << 20),
        name="pack_targets",
    )(me, owners, queries, out_grads)
    return outs[0], outs[1 : 1 + half], outs[1 + half :]


def hold_kernel(count, *refs):
    for x_ref, out_ref in zip(refs[:count], refs[-count:]):
        out_ref[...] = x_ref[...]


def hold(arrays, earlier):
    return pl.pallas_call(
        functools.partial(hold_kernel, len(arrays)),
        out_shape=[jax.ShapeDtypeStruct(x.shape, x.dtype) for x in arrays],
        in_specs=[VMEM_SPEC] * len(arrays) + [ANY_SPEC] * len(earlier),
        out_specs=[VMEM_SPEC] * len(arrays),
        compiler_params=pltpu.CompilerParams(vmem_limit_bytes=VMEM_BYTES),
        cost_estimate=cost(0, 1 << 20),
        name="hold",
    )(*arrays, *earlier)


def token(arrays):
    return sum(x.reshape(-1, x.shape[-1])[:1, :LANES].astype(F32) for x in arrays)


def join_kernel(near0, near1, over0, over1, *refs):
    first_ref, second_ref = refs[-2:]
    first_ref[0], first_ref[1] = near0[0], near1[0]
    second_ref[0], second_ref[1] = over0[1], over1[1]


def join(near, over, earlier):
    shape = jax.ShapeDtypeStruct(near[0].shape, BF16)
    return pl.pallas_call(
        join_kernel,
        out_shape=[shape] * 2,
        in_specs=[VMEM_SPEC] * 4 + [ANY_SPEC] * len(earlier),
        out_specs=[VMEM_SPEC] * 2,
        compiler_params=pltpu.CompilerParams(vmem_limit_bytes=VMEM_BYTES),
        cost_estimate=cost(0, 1 << 20),
        name="join",
    )(*near, *over, *earlier)


def merge_kernel(half, *refs):
    blocks, got_refs, out_refs = refs[:half], refs[half : 2 * half], refs[-half:]
    for d in range(half):
        out_refs[d][0] = blocks[d][...]
        out_refs[d][1] = got_refs[d][...]


def merge(blocks, got, earlier):
    half = len(blocks)
    return pl.pallas_call(
        functools.partial(merge_kernel, half),
        out_shape=[jax.ShapeDtypeStruct((2,) + blocks[0].shape, BF16)] * half,
        in_specs=[VMEM_SPEC] * (2 * half) + [ANY_SPEC] * len(earlier),
        out_specs=[VMEM_SPEC] * half,
        compiler_params=pltpu.CompilerParams(vmem_limit_bytes=VMEM_BYTES),
        cost_estimate=cost(0, 1 << 20),
        name="merge",
    )(*blocks, *got, *earlier)


def unpack_kernel(peers, per_peer, table_ref, *refs):
    half = peers // 2
    near_refs, over_ref, out_ref = refs[:half], refs[half], refs[half + 1]
    near_s, over_s, rows_ref, sems = refs[half + 2 :]
    targets, rows, width = out_ref.shape
    block_rows = per_peer * rows
    copies = fetch(
        list(near_refs) + [over_ref], [near_s.at[d] for d in range(half)] + [over_s], sems
    )
    for copy in copies:
        copy.wait()
    for d in range(peers):
        block = near_s[d, :block_rows] if d < half else over_s[d - half]
        rows_ref[d * per_peer : (d + 1) * per_peer] = block.astype(F32).reshape(
            per_peer, rows, width
        )

    def move(slot, _):
        t = table_ref[slot]

        @pl.when(t < targets)
        def _():
            out_ref[t] = rows_ref[slot].astype(BF16)

        return 0

    lax.fori_loop(0, peers * per_peer, move, 0)


def unpack(table, near, over, targets, rows, per_peer):
    half, width = len(near), near[0].shape[1]
    return pl.pallas_call(
        functools.partial(unpack_kernel, 2 * half, per_peer),
        out_shape=jax.ShapeDtypeStruct((targets, rows, width), BF16),
        in_specs=[SMEM_SPEC] + [ANY_SPEC] * (half + 1),
        out_specs=VMEM_SPEC,
        scratch_shapes=[
            pltpu.VMEM((half,) + near[0].shape, BF16),
            pltpu.VMEM(over.shape, BF16),
            pltpu.VMEM((2 * half * per_peer, rows, width), F32),
            pltpu.SemaphoreType.DMA((half + 1,)),
        ],
        compiler_params=pltpu.CompilerParams(vmem_limit_bytes=VMEM_BYTES),
        cost_estimate=cost(0, 3 << 20),
        name="unpack_query_grads",
    )(table, *near, over)


def attend_kernel(peers, chunk, chunks, waits, len_ref, k_hbm, v_hbm, *refs):
    half = peers // 2
    in_refs, before_refs = refs[:half], refs[half : half + chunk]
    groups = k_hbm.shape[1] // (chunks * LANES)
    outs = refs[half + chunk + waits : -9]
    kv_ref, out_refs = outs[0], outs[1:]
    q_s, g_s, o_s, kt_s, kg_s, vg_s, k_ref, v_ref, sems = refs[-9:]
    src_len = k_ref.shape[0]
    copies = fetch([k_hbm, v_hbm], [k_ref, v_ref], sems)
    _, per_peer, double, _ = in_refs[0].shape
    width = groups * LANES
    rows = double // 2
    block_rows = per_peer * rows
    total_rows = peers * block_rows
    tile = min(1024, total_rows)
    scale = HEAD_DIM**-0.5
    for d in range(peers):
        at = slice(d * block_rows, (d + 1) * block_rows)
        for a in range(groups):
            lane, mine = (a * chunks + chunk) * LANES, slice(a * LANES, (a + 1) * LANES)
            both = in_refs[d // 2][d % 2, :, :, lane : lane + LANES].astype(F32)
            q_s[at, mine] = (both[:, :rows] * scale).reshape(block_rows, LANES).astype(BF16)
            g_s[at, mine] = both[:, rows:].reshape(block_rows, LANES).astype(BF16)
    for copy in copies:
        copy.wait()
    valid = lax.broadcasted_iota(jnp.int32, (src_len, 1), 0) < len_ref[0]
    lane_head = lax.broadcasted_iota(jnp.int32, (1, LANES), 1) // HEAD_DIM
    for a in range(groups):
        lane = (a * chunks + chunk) * LANES
        mine = slice(a * LANES, (a + 1) * LANES)
        kt_s[...] = (k_ref[:, lane : lane + LANES].astype(F32) * scale).T.astype(BF16)
        kg_s[...] = jnp.zeros_like(kg_s)
        vg_s[...] = jnp.zeros_like(vg_s)

        def step(i, _, lane=lane, mine=mine):
            at = pl.ds(pl.multiple_of(i * tile, tile), tile)
            q_pair, g_pair = q_s[at, mine], g_s[at, mine]
            k_pair, v_pair = k_ref[:, lane : lane + LANES], v_ref[:, lane : lane + LANES]
            parts = []
            for h in range(LANES // HEAD_DIM):
                q_h = jnp.where(lane_head == h, q_pair, jnp.zeros_like(q_pair))
                g_h = jnp.where(lane_head == h, g_pair, jnp.zeros_like(g_pair))
                scores = lax.dot_general(k_pair, q_h, NT, preferred_element_type=F32)
                scores = jnp.where(valid, scores, -1e30)
                prob_grad = lax.dot_general(v_pair, g_h, NT, preferred_element_type=F32)
                peak = jnp.max(scores, axis=0, keepdims=True)
                terms = jnp.exp(scores - peak)
                probs = terms * (1.0 / jnp.sum(terms, axis=0, keepdims=True))
                row_delta = jnp.sum(probs * prob_grad, axis=0, keepdims=True)
                score_grad = (probs * (prob_grad - row_delta)).astype(BF16)
                vg_s[...] += jnp.dot(probs.astype(BF16), g_h, preferred_element_type=F32)
                kg_s[...] += jnp.dot(score_grad, q_h, preferred_element_type=F32)
                parts.append(
                    jnp.dot(
                        kt_s[h * HEAD_DIM : (h + 1) * HEAD_DIM],
                        score_grad,
                        preferred_element_type=F32,
                    )
                )
            o_s[at, mine] = jnp.concatenate(parts, axis=0).T.astype(BF16)
            return 0

        lax.fori_loop(0, total_rows // tile, step, 0)
        kv_ref[a, :, :LANES] = kg_s[...].astype(BF16)
        kv_ref[a, :, LANES:] = vg_s[...].astype(BF16)
    if chunk < chunks - 1:
        out_refs[0][...] = o_s[...]
        return
    for d in range(half):
        at = slice(2 * d * block_rows, 2 * (d + 1) * block_rows)
        for c, part_ref in enumerate((*before_refs, o_s)):
            for a in range(groups):
                lane = (a * chunks + c) * LANES
                out_refs[d][:, lane : lane + LANES] = part_ref[at, a * LANES : (a + 1) * LANES]


def attend(length, keys, values, blocks, before, earlier):
    chunk, chunks = len(before), CHUNKS
    half = len(blocks)
    peers = 2 * half
    src_len, width = keys.shape
    _, per_peer, double, _ = blocks[0].shape
    part = width // chunks
    block_rows = per_peer * double // 2
    total_rows = peers * block_rows
    groups = part // LANES
    heads = part // HEAD_DIM
    query_shapes = [jax.ShapeDtypeStruct((total_rows, part), BF16)]
    if chunk == chunks - 1:
        query_shapes = [jax.ShapeDtypeStruct((2 * block_rows, width), BF16)] * half
    outs = pl.pallas_call(
        functools.partial(attend_kernel, peers, chunk, chunks, len(earlier)),
        out_shape=[jax.ShapeDtypeStruct((groups, src_len, 2 * LANES), BF16)] + query_shapes,
        in_specs=[SMEM_SPEC, HBM_SPEC, HBM_SPEC] + [VMEM_SPEC] * (half + chunk + len(earlier)),
        out_specs=[VMEM_SPEC] * (1 + len(query_shapes)),
        scratch_shapes=[
            pltpu.VMEM((total_rows, part), BF16),
            pltpu.VMEM((total_rows, part), BF16),
            pltpu.VMEM((total_rows, part), BF16),
            pltpu.VMEM((LANES, src_len), BF16),
            pltpu.VMEM((src_len, LANES), F32),
            pltpu.VMEM((src_len, LANES), F32),
            pltpu.VMEM(keys.shape, BF16),
            pltpu.VMEM(values.shape, BF16),
            pltpu.SemaphoreType.DMA((2,)),
        ],
        compiler_params=pltpu.CompilerParams(vmem_limit_bytes=ATTEND_BYTES),
        cost_estimate=cost(
            40 * total_rows * src_len * HEAD_DIM * heads, 4 << 20, total_rows * src_len * heads
        ),
        name="attend",
    )(length, keys, values, *blocks, *before, *earlier)
    return outs[0], outs[1:]


def weight_kernel(count, first, place_ref, states_ref, *refs):
    own_ref, sib_ref, states_s, blocks_s, sems = refs[-5:]
    copies = fetch(
        [states_ref] + list(refs[:count]), [states_s] + [blocks_s.at[i] for i in range(count)], sems
    )
    copies[0].wait()
    states = states_s[...]
    tall = blocks_s.shape[-1]
    for i in range(count):
        copies[1 + i].wait()
        for k in range(2):
            index, c = (2 * (i // 2) + k, i % 2) if first == 0 else (first + i, k)
            piece = lax.dot_general(blocks_s[i, k], states, TN, preferred_element_type=F32)
            away, seq = place_ref[2 * index], place_ref[2 * index + 1]
            at = slice(c * tall, (c + 1) * tall)

            @pl.when(away == 0)
            def _(piece=piece, seq=seq, at=at):
                own_ref[seq, at] = piece

            @pl.when(away != 0)
            def _(piece=piece, seq=seq, at=at):
                sib_ref[seq, at] = piece.astype(BF16)


def weight_parts(place, states, blocks, first, seq_size, totals=(), earlier=()):
    src_len, width = states.shape
    tall = 2 * blocks[0].shape[-1]
    shape = (seq_size, tall, width)
    given = 2 + len(blocks)
    return pl.pallas_call(
        functools.partial(weight_kernel, len(blocks), first),
        out_shape=[jax.ShapeDtypeStruct(shape, F32), jax.ShapeDtypeStruct(shape, BF16)],
        in_specs=[SMEM_SPEC, HBM_SPEC]
        + [ANY_SPEC] * len(blocks)
        + [VMEM_SPEC] * len(totals)
        + [ANY_SPEC] * len(earlier),
        out_specs=[VMEM_SPEC] * 2,
        input_output_aliases={given + i: i for i in range(len(totals))},
        scratch_shapes=[
            pltpu.VMEM((src_len, width), BF16),
            pltpu.VMEM((len(blocks),) + blocks[0].shape, BF16),
            pltpu.SemaphoreType.DMA((1 + len(blocks),)),
        ],
        compiler_params=pltpu.CompilerParams(vmem_limit_bytes=VMEM_BYTES),
        cost_estimate=cost(8 * len(blocks) * src_len * tall * width, 6 << 20),
        name="weight_parts",
    )(place, states, *blocks, *totals, *earlier)


def combine_kernel(pieces, seq_ref, own_ref, got_ref, *refs):
    for d, out_ref in enumerate(refs[-pieces:]):
        index = seq_ref[0] ^ d
        total = own_ref[index] + got_ref[index].astype(F32)
        out_ref[...] = total.astype(out_ref.dtype)


def combine(seq, own, got, earlier):
    pieces, *shape = own.shape
    return pl.pallas_call(
        functools.partial(combine_kernel, pieces),
        out_shape=[jax.ShapeDtypeStruct(shape, F32)]
        + [jax.ShapeDtypeStruct(shape, BF16)] * (pieces - 1),
        in_specs=[SMEM_SPEC] + [VMEM_SPEC] * 2 + [ANY_SPEC] * len(earlier),
        out_specs=[VMEM_SPEC] * pieces,
        compiler_params=pltpu.CompilerParams(vmem_limit_bytes=VMEM_BYTES),
        cost_estimate=cost(0, 6 << 20),
        name="combine",
    )(seq, own, got, *earlier)


def state_kernel(pieces, order_ref, *refs):
    in_refs, out_ref = refs[: 8 + pieces], refs[8 + pieces]
    total_ref, w_s, blocks_s, sems = refs[9 + pieces :]
    targets = [blocks_s.at[i] for i in range(8)]
    copies = fetch(in_refs, [w_s.at[i] for i in range(pieces)] + targets, sems)
    for copy in copies:
        copy.wait()
    total_ref[...] = jnp.zeros_like(total_ref)
    for index in range(8):
        e, a = index // 2, index % 2
        piece = order_ref[index]
        for c in range(2):
            at = slice(c * LANES, (c + 1) * LANES)
            weight = jnp.concatenate([w_s[piece, 0, at], w_s[piece, 1, at]], axis=0)
            block = blocks_s[2 * e + c, a] if e < 3 else blocks_s[6 + a, c]
            total_ref[...] += jnp.dot(block, weight, preferred_element_type=F32)
    out_ref[...] = total_ref[...].astype(BF16)


def state_grads(order, weights, blocks):
    src_len = blocks[0].shape[1]
    pieces, width = len(weights), weights[0].shape[-1]
    return pl.pallas_call(
        functools.partial(state_kernel, pieces),
        out_shape=jax.ShapeDtypeStruct((src_len, width), BF16),
        in_specs=[SMEM_SPEC] + [ANY_SPEC] * (pieces + len(blocks)),
        out_specs=VMEM_SPEC,
        scratch_shapes=[
            pltpu.VMEM((src_len, width), F32),
            pltpu.VMEM((pieces,) + weights[0].shape, BF16),
            pltpu.VMEM((len(blocks),) + blocks[0].shape, BF16),
            pltpu.SemaphoreType.DMA((pieces + len(blocks),)),
        ],
        compiler_params=pltpu.CompilerParams(vmem_limit_bytes=ATTEND_BYTES),
        cost_estimate=cost(32 * src_len * 2 * LANES * width, 8 << 20),
        name="state_grads",
    )(order, *weights, *blocks)


def swap(x, axes, size, distance):
    return lax.ppermute(x, axes, [(i, i ^ distance) for i in range(size)])


def ring(x):
    size = lax.axis_size("seq")
    return lax.ppermute(x, "seq", [(z, (z + 1) % size) for z in range(size)])


def exchange(blocks, sib, earlier):
    half = len(blocks)
    got = [swap(x, "grp", 2, 1) for x in sib]
    pairs = merge(blocks, got, earlier)
    line = {d: swap(pairs[d], "seq", half, d) for d in range(half - 1, 0, -1)}
    return [pairs[0]] + [line[d] for d in range(1, half)], pairs[1:]


def send_back(pairs):
    half, rows = len(pairs), pairs[0].shape[0] // 2
    line = {d: swap(pairs[d], "seq", half, d) for d in range(half - 1, 0, -1)}
    near = [pairs[0]] + [line[d] for d in range(1, half)]
    return near, swap(jnp.stack([pair[rows:] for pair in near]), "grp", 2, 1)


def block_grads(query_block, grad_block, key_local, value_local, key_valid):
    score_scale = key_local.shape[-1] ** (-0.5)
    scores = (
        jnp.einsum("rhe,khe->hrk", query_block, key_local, preferred_element_type=jnp.float32)
        * score_scale
    )
    scores = jnp.where(key_valid[None, None, :], scores, -1e30)
    row_peak = jnp.max(scores, axis=-1, keepdims=True)
    exp_terms = jnp.exp(scores - row_peak)
    attn_probs = exp_terms / jnp.sum(exp_terms, axis=-1, keepdims=True)
    probs_b = attn_probs.astype(jnp.bfloat16)
    context = jnp.einsum("hrk,khe->rhe", probs_b, value_local, preferred_element_type=jnp.float32)
    row_delta = jnp.sum(grad_block.astype(jnp.float32) * context, axis=-1)
    prob_grad = jnp.einsum(
        "rhe,khe->hrk", grad_block, value_local, preferred_element_type=jnp.float32
    )
    score_grad = (attn_probs * (prob_grad - row_delta.T[:, :, None]) * score_scale).astype(
        jnp.bfloat16
    )
    query_grad = jnp.einsum(
        "hrk,khe->rhe", score_grad, key_local, preferred_element_type=jnp.float32
    ).astype(jnp.bfloat16)
    key_grad = jnp.einsum(
        "hrk,rhe->khe", score_grad, query_block, preferred_element_type=jnp.float32
    )
    value_grad = jnp.einsum("hrk,rhe->khe", probs_b, grad_block, preferred_element_type=jnp.float32)
    return (query_grad, key_grad, value_grad)


def any_mesh(queries, out_grads, owners, src_keys, src_values, states, kv_weight, src_lengths):
    peer_count = lax.axis_size(("grp", "seq"))
    tgt_dev, tgt_len, inner_dev = queries.shape
    per_peer = max(2, 2 * tgt_dev // peer_count)
    slot_count = peer_count * per_peer
    row_width = tgt_len * inner_dev
    head_dim = HEAD_DIM
    local_heads = inner_dev // head_dim
    src_len = src_keys.shape[1]
    member = (owners[:, None] == jnp.arange(peer_count, dtype=jnp.int32)[None, :]).astype(jnp.int32)
    earlier = jnp.cumsum(member, axis=0) - member
    rank_own = jnp.sum(earlier * member, axis=1)
    slot_of = owners * per_peer + rank_own
    selector = (jnp.arange(slot_count, dtype=jnp.int32)[:, None] == slot_of[None, :]).astype(
        jnp.bfloat16
    )
    send_query = jnp.dot(
        selector, queries.reshape(tgt_dev, row_width), preferred_element_type=jnp.float32
    ).astype(jnp.bfloat16)
    send_grad = jnp.dot(
        selector, out_grads.reshape(tgt_dev, row_width), preferred_element_type=jnp.float32
    ).astype(jnp.bfloat16)
    got_query, got_grad = (
        lax.all_to_all(send_query, ("grp", "seq"), split_axis=0, concat_axis=0, tiled=True),
        lax.all_to_all(send_grad, ("grp", "seq"), split_axis=0, concat_axis=0, tiled=True),
    )
    total_rows = slot_count * tgt_len
    block_rows = 512
    block_count = total_rows // block_rows
    query_rows = got_query.reshape(block_count, block_rows, local_heads, head_dim)
    grad_rows = got_grad.reshape(block_count, block_rows, local_heads, head_dim)
    key_local = src_keys[0].reshape(src_len, local_heads, head_dim)
    value_local = src_values[0].reshape(src_len, local_heads, head_dim)
    key_valid = jnp.arange(src_len, dtype=jnp.int32) < src_lengths[0]

    def attend_step(totals, block_pair):
        query_grad, key_grad, value_grad = block_grads(
            block_pair[0], block_pair[1], key_local, value_local, key_valid
        )
        return ((totals[0] + key_grad, totals[1] + value_grad), query_grad)

    zero_grads = jnp.zeros((src_len, local_heads, head_dim), jnp.float32)
    (key_total, value_total), query_blocks = lax.scan(
        attend_step, (zero_grads, zero_grads), (query_rows, grad_rows)
    )
    back_rows = query_blocks.reshape(slot_count, row_width)
    returned = lax.all_to_all(back_rows, ("grp", "seq"), split_axis=0, concat_axis=0, tiled=True)
    query_out = lax.dot_general(
        selector, returned, (((0,), (0,)), ((), ())), preferred_element_type=jnp.float32
    )
    query_out = query_out.astype(jnp.bfloat16).reshape(tgt_dev, tgt_len, inner_dev)
    key_bf = key_total.reshape(src_len, inner_dev).astype(jnp.bfloat16)
    value_bf = value_total.reshape(src_len, inner_dev).astype(jnp.bfloat16)
    key_all, value_all = (
        lax.all_gather(key_bf, "mdl", axis=1, tiled=True),
        lax.all_gather(value_bf, "mdl", axis=1, tiled=True),
    )
    weight_piece = lax.all_gather(kv_weight, ("grp", "seq"), axis=0, tiled=True)
    key_cols = key_all
    value_cols = value_all
    total = jnp.dot(key_cols, weight_piece[:, 0, :], preferred_element_type=jnp.float32)
    state_sum = total + jnp.dot(
        value_cols, weight_piece[:, 1, :], preferred_element_type=jnp.float32
    )
    state_out = state_sum.astype(jnp.bfloat16).reshape(1, src_len, kv_weight.shape[2])
    flat_states = states.reshape(src_len, states.shape[2])
    key_cols = key_all
    value_cols = value_all
    grad_key = lax.dot_general(
        key_cols, flat_states, (((0,), (0,)), ((), ())), preferred_element_type=jnp.float32
    )
    grad_value = lax.dot_general(
        value_cols, flat_states, (((0,), (0,)), ((), ())), preferred_element_type=jnp.float32
    )
    weight_out = lax.psum_scatter(
        jnp.stack([grad_key, grad_value], axis=1), ("grp", "seq"), scatter_dimension=0, tiled=True
    )
    return (query_out, state_out, weight_out)


def on_device(queries, out_grads, owners, src_keys, src_values, states, kv_weight, src_lengths):
    seq_size = lax.axis_size("seq")
    peers = lax.axis_size(PEERS)
    targets, rows, width = queries.shape
    per_peer = max(2, 2 * targets // peers)
    src_len = src_keys.shape[1]
    chunks = CHUNKS
    groups = 2
    me = lax.axis_index(PEERS).astype(jnp.int32)
    mdl = lax.axis_index("mdl").astype(jnp.int32)
    grp = lax.axis_index("grp").astype(jnp.int32)
    keys, values = src_keys[0], src_values[0]
    flat_states = states[0]
    source = mdl ^ (jnp.arange(4 * groups, dtype=jnp.int32) // groups)
    order = source * groups + jnp.arange(4 * groups, dtype=jnp.int32) % groups
    seq = lax.axis_index("seq").astype(jnp.int32)
    weight_order = ((order // seq_size) ^ grp) * seq_size + (seq - order) % seq_size
    place = jnp.stack([(order // seq_size) ^ grp, order % seq_size], axis=1).reshape(-1)

    tall = jnp.transpose(kv_weight, (1, 0, 2))
    lines = [tall, ring(tall)]
    table, blocks, sib = pack(me[None], owners, queries, out_grads, peers, per_peer, 0, 1)
    got, _ = exchange(blocks, sib, lines[1:])
    lines.append(ring(hold(lines[1:], got[1:])[0]))
    lines.append(ring(lines[2]))
    first, before = attend(src_lengths, keys, values, got, [], [])
    near, over = [swap(first, "mdl", 4, 1)], [swap(first, "mdl", 4, 2)]
    second, query_blocks = attend(src_lengths, keys, values, got, before, [token(lines[2:3])])
    back, other = send_back(query_blocks)
    second = hold([second], [near[0], over[0], lines[3]])[0]
    near.append(swap(second, "mdl", 4, 1))
    over.append(swap(second, "mdl", 4, 2))
    across = join(near, over, [])
    across = [swap(across[0], "mdl", 4, 2), swap(across[1], "mdl", 4, 1)]
    gathered = [first, second, *near, *over, *across]
    totals = weight_parts(place, flat_states, gathered[:6], 0, seq_size, (), [])
    own, sib = weight_parts(
        place, flat_states, gathered[6:], 6, seq_size, totals, back[1:]
    )
    keep, *sends = combine(seq[None], own, swap(sib, "grp", 2, 1), [])
    line = [swap(sends[d - 1], "seq", seq_size, d) for d in range(seq_size - 1, 0, -1)]
    weight_sum = keep + sum(x.astype(F32) for x in line)
    lines = lines + [swap(x, "grp", 2, 1) for x in lines]
    state_out = state_grads(weight_order, lines, gathered)
    query_out = unpack(table, back, other, targets, rows, per_peer)
    weight_out = weight_sum.reshape(2, 2, LANES, width).transpose(0, 2, 1, 3)
    weight_out = weight_out.reshape(2 * LANES, 2, width)
    return (query_out, state_out.reshape(1, src_len, width), weight_out)


def solution(mesh):
    spec = P(PEERS, None, "mdl")
    in_specs = (spec, spec, P(PEERS), spec, spec, spec, spec, P(PEERS))
    tuned = (mesh.shape["grp"], mesh.shape["seq"], mesh.shape["mdl"]) == (2, 4, 4)
    return jax.shard_map(
        on_device if tuned else any_mesh, mesh=mesh, in_specs=in_specs, out_specs=(spec, spec, spec), check_vma=False
    )
```
